32 devices in a mesh: grp: 2 (over x), chol: 16 (over z, y, core).
Axes of the slice: x: 2, y: 2, z: 4, core: 2. Of those that a mesh axis runs over, the one named last changes fastest.
Arguments:
- walkers: bfloat16 [1024, 64, 256], P(('grp', 'chol')), parts along dimension 0, may hold values from -6 to 6
- fields: bfloat16 [1024, 1024], P(('grp', 'chol')), parts along dimension 0, may hold values from -6 to 6
- chol_vectors: bfloat16 [1024, 256, 256], P(None, 'chol'), may hold values from -0.375 to 0.375
- rotated: bfloat16 [1024, 64, 256], P(None, 'chol'), may hold values from -0.046875 to 0.046875
- send_walker: int32 [32, 16, 2], P(('grp', 'chol')), parts along dimension 0, may hold values from -1 to 31, as said below
- slot_row: int32 [1024], P(('grp', 'chol')), parts along dimension 0, may hold values from 0 to 31, as said below
Outputs:
- new_walkers: bfloat16 [1024, 64, 256], P(('grp', 'chol')), parts along dimension 0
- force_bias: float32 [1024, 1024], P(('grp', 'chol')), parts along dimension 0
The draws below stay inside these ranges and needn't reach their ends.
There are 2 independent parts, one for each index of `grp`. The reference program is written for one: setup_inputs(seed, part) draws one part's arguments, and reference() takes and returns one part's arrays. A program takes and returns all parts, laid end to end along the dimension named above; an argument that names none is the same for every part. Nothing has to cross between parts.
Inputs may be any that keep to these rules, and one draw needn't show every extreme that they name: `send_walker`: entry [s, d, c] is the index, among the 32 walkers of block s, of the walker that block s sends as its c-th one to block d, or -1 where it sends none; indices of one [s, d] row come first, -1 after. Some pair of blocks uses all 2 entries. `slot_row`: for every slot of block d, s * 2 + c names a valid entry [s, d, c] of send_walker, and every valid entry is named by exactly one slot of block d.
All inputs are finite; a program needn't handle non-finite values.
Results may differ from the reference program's by a relative error of at most 0.0075.
Values may be sent and summed in bfloat16 or wider, within the bound.
No kernel may reach another device: no remote copies, remote signals or barrier semaphores. Data moves between devices by JAX's collectives and lax.ppermute only.
A program may use at most 64 MiB of HBM per device.

```python
import math
import jax
import jax.numpy as jnp
from jax import lax

M = 256
N = 64
NCHOL = 1024
CAP = 2
W_DEV = 32
BLOCKS = 16
WALKERS = 512


def branch_plan(key):
    base = jax.random.fold_in(key, 4111)
    offset = jax.random.randint(jax.random.fold_in(base, 1), (), 0, BLOCKS)
    dest_keys = jax.random.split(jax.random.fold_in(base, 2), BLOCKS)

    def one_dest(dest_key, dest):
        key_a, key_b, key_c = jax.random.split(dest_key, 3)
        doubled = (dest + offset) % BLOCKS
        order = jax.random.permutation(key_a, 2 * (BLOCKS - 1)) % (BLOCKS - 1)
        others = jnp.where(order >= doubled, order + 1, order)[:W_DEV - 2]
        sources = jnp.concatenate([jnp.stack([doubled, doubled]), others]).astype(jnp.int32)
        sources = sources[jax.random.permutation(key_b, W_DEV)]
        walker_index = jax.random.randint(key_c, (W_DEV,), 0, W_DEV).astype(jnp.int32)
        positions = jnp.arange(W_DEV, dtype=jnp.int32)
        same = (sources[:, None] == sources[None, :]) & (positions[None, :] < positions[:, None])
        rank = jnp.sum(same.astype(jnp.int32), axis=1).astype(jnp.int32)
        return (sources, rank, walker_index)
    sources, rank, walker_index = jax.vmap(one_dest)(dest_keys, jnp.arange(BLOCKS, dtype=jnp.int32))
    dest_grid = jnp.broadcast_to(jnp.arange(BLOCKS, dtype=jnp.int32)[:, None], (BLOCKS, W_DEV))
    table = jnp.full((BLOCKS, BLOCKS, CAP), -1, jnp.int32)
    table = table.at[sources.reshape(-1), dest_grid.reshape(-1), rank.reshape(-1)].set(walker_index.reshape(-1))
    rows = (sources * CAP + rank).reshape(-1).astype(jnp.int32)
    return (table, rows)


def draw_send_walker(key, part):
    return branch_plan(key)[0]


def draw_slot_row(key, part):
    return branch_plan(key)[1]


def block_scale(rng, shape, pieces, least, largest):
    loudness = 1.0
    for axis_at, blocks in pieces:
        steps = jax.random.uniform(jax.random.fold_in(jax.random.fold_in(rng, 6), axis_at), (blocks,), jnp.float32, least / len(pieces), largest / len(pieces))
        loudness = loudness * jnp.repeat(jnp.exp(steps), shape[axis_at] // blocks).reshape((-1,) + (1,) * (len(shape) - 1 - axis_at))
    return loudness


def bell_draw(key, shape, spread, bound, pieces=(), kind=jnp.bfloat16):
    array = jax.random.normal(key, shape, jnp.float32) * spread
    if len(pieces) > 0:
        array = block_scale(key, shape, pieces, -0.22, 0.18) * array
    return jnp.clip(array, min=-bound, max=bound).astype(kind)


def setup_inputs(seed: int = 0, part: int = 0) -> dict:
    key_list = jax.random.split(jax.random.key(seed), 7)
    part_splits = jax.random.split(jax.random.fold_in(key_list[6], part), 7)
    walkers = bell_draw(part_splits[0], (WALKERS, N, M), 1.0, 6.0, ((0, 16),))
    fields = bell_draw(part_splits[1], (WALKERS, NCHOL), 1.0, 6.0, ((0, 16),))
    chol_vectors = bell_draw(key_list[2], (NCHOL, M, M), M ** -0.5, 0.375, ((1, 16),))
    rotated = bell_draw(key_list[3], (NCHOL, N, M), (N * M) ** -0.5, 0.046875, ((1, 16),))
    send_walker = draw_send_walker(jax.random.fold_in(jax.random.fold_in(key_list[6], part), 71), part)
    slot_row = draw_slot_row(jax.random.fold_in(jax.random.fold_in(key_list[6], part), 71), part)
    return dict(walkers=walkers, fields=fields, chol_vectors=chol_vectors, rotated=rotated, send_walker=send_walker, slot_row=slot_row)


field_scale = 1.5

def reference(walkers, fields, chol_vectors, rotated, send_walker, slot_row):
    dest = jnp.arange(WALKERS, dtype=jnp.int32) // W_DEV
    source = (slot_row // CAP).astype(jnp.int32)
    rank = (slot_row % CAP).astype(jnp.int32)
    local_index = send_walker[source, dest, rank].astype(jnp.int32)
    parent = (source * W_DEV + local_index).astype(jnp.int32)
    branched = walkers[parent]
    chol_flat = chol_vectors.reshape(NCHOL, M * M)
    rot_flat = rotated.reshape(NCHOL, N * M)
    scale = field_scale / math.sqrt(NCHOL)

    def propagate(blocks):
        field_rows, phi_block = blocks
        operator = (jnp.dot(field_rows, chol_flat, preferred_element_type=jnp.float32) * scale).astype(jnp.bfloat16)
        operator = operator.reshape(W_DEV, M, M)
        total = phi_block.astype(jnp.float32)
        term = phi_block
        for degree in range(1, 6):
            product = jnp.einsum('waj,wij->wai', term.astype(jnp.float32), operator.astype(jnp.float32))
            term = (product / degree).astype(jnp.bfloat16)
            total = total + term.astype(jnp.float32)
        new_block = total.astype(jnp.bfloat16)
        bias = lax.dot_general(new_block.reshape(W_DEV, N * M), rot_flat, (((1,), (1,)), ((), ())), preferred_element_type=jnp.float32)
        return (new_block, bias)
    new_all, bias_all = lax.map(propagate, (fields.reshape(BLOCKS, W_DEV, NCHOL), branched.reshape(BLOCKS, W_DEV, N, M)))
    return (new_all.reshape(WALKERS, N, M), bias_all.reshape(WALKERS, NCHOL))
```

```python
import functools
import math

import jax
import jax.numpy as jnp
import numpy as np
from jax import lax
from jax.experimental import pallas as pl
from jax.experimental.pallas import tpu as pltpu
from jax.sharding import PartitionSpec as P

field_scale = 1.5
degrees = 5
inner = 4


def branch_walkers(walkers, send_walker, slot_row):
    slots, electrons, orbitals = walkers.shape
    flat_walkers = walkers.reshape(slots, electrons * orbitals)
    send_list = send_walker.reshape(-1)
    choose_send = (send_list[:, None] == jnp.arange(slots, dtype=jnp.int32)[None, :]).astype(
        jnp.bfloat16
    )
    outgoing = jnp.dot(choose_send, flat_walkers, preferred_element_type=jnp.float32).astype(
        jnp.bfloat16
    )
    incoming = lax.all_to_all(outgoing, "chol", split_axis=0, concat_axis=0, tiled=True)
    choose_recv = (
        slot_row[:, None] == jnp.arange(incoming.shape[0], dtype=jnp.int32)[None, :]
    ).astype(jnp.bfloat16)
    branched = jnp.dot(choose_recv, incoming, preferred_element_type=jnp.float32).astype(
        jnp.bfloat16
    )
    return branched.reshape(slots, electrons, orbitals)


def build_operators(fields, chol_vectors):
    nchol, row_local, orbitals = chol_vectors.shape
    chol_flat = chol_vectors.reshape(nchol, row_local * orbitals)
    scale = field_scale / math.sqrt(nchol)
    all_fields = lax.all_gather(fields, "chol", axis=0, tiled=True)
    all_rows = (jnp.dot(all_fields, chol_flat, preferred_element_type=jnp.float32) * scale).astype(
        jnp.bfloat16
    )
    return all_rows.reshape(all_rows.shape[0], row_local, orbitals)


def plain_shards(walkers, fields, chol_vectors, rotated, send_walker, slot_row):
    slots, electrons, orbitals = walkers.shape
    branched = branch_walkers(walkers, send_walker, slot_row)
    operator_rows = build_operators(fields, chol_vectors)
    operator = lax.all_to_all(operator_rows, "chol", split_axis=0, concat_axis=1, tiled=True)
    total = branched.astype(jnp.float32)
    term = branched
    for degree in range(1, degrees + 1):
        product = jnp.einsum("waj,wij->wai", term, operator, preferred_element_type=jnp.float32)
        term = (product / degree).astype(jnp.bfloat16)
        total = total + term.astype(jnp.float32)
    new_walkers = total.astype(jnp.bfloat16)
    nchol, elec_local, _ = rotated.shape
    electron_rows = lax.all_to_all(new_walkers, "chol", split_axis=1, concat_axis=0, tiled=True)
    electron_flat = electron_rows.reshape(electron_rows.shape[0], elec_local * orbitals)
    rot_flat = rotated.reshape(nchol, elec_local * orbitals)
    force_bias = lax.psum_scatter(
        lax.dot_general(
            electron_flat, rot_flat, (((1,), (1,)), ((), ())), preferred_element_type=jnp.float32
        ),
        "chol",
        scatter_dimension=0,
        tiled=True,
    )
    return (new_walkers, force_bias)


def propagate_kernel(pieces, planes, rows, elec, place_ref, phi_ref, *refs):
    piece_refs = refs[:pieces]
    new_ref = refs[pieces]
    part_refs = refs[pieces + 1 : pieces + 1 + planes]
    op_ref, done_ref = refs[pieces + 1 + planes :]
    block = phi_ref.shape[0]
    for r in range(pieces):
        at = pl.multiple_of(place_ref[r] * rows, rows)
        op_ref[:, pl.ds(at, rows), :] = piece_refs[r][...]
    terms = [phi_ref[w] for w in range(block)]
    totals = [t.astype(jnp.float32) for t in terms]
    for degree in range(1, degrees + 1):
        for w in range(block):
            product = lax.dot_general(
                terms[w], op_ref[w], (((1,), (1,)), ((), ())), preferred_element_type=jnp.float32
            )
            terms[w] = (product * np.float32(1.0 / degree)).astype(jnp.bfloat16)
            totals[w] = totals[w] + terms[w].astype(jnp.float32)
    for w in range(block):
        out = totals[w].astype(jnp.bfloat16)
        new_ref[w] = out
        done_ref[w] = out
    for k in range(planes):
        at = pl.multiple_of(place_ref[pieces + k] * elec, elec)
        part_refs[k][...] = done_ref[:, pl.ds(at, elec), :]


def propagate(phi, pieces, place, planes):
    slots, electrons, orbitals = phi.shape
    rows = pieces[0].shape[1]
    elec = electrons // planes
    block = 4 if slots % 4 == 0 else 1
    spec = lambda height: pl.BlockSpec((block, height, orbitals), lambda i: (i, 0, 0))
    shape = lambda height: jax.ShapeDtypeStruct((slots, height, orbitals), jnp.bfloat16)
    outs = pl.pallas_call(
        functools.partial(propagate_kernel, len(pieces), planes, rows, elec),
        grid=(slots // block,),
        in_specs=[pl.BlockSpec(memory_space=pltpu.SMEM), spec(electrons)]
        + [spec(rows)] * len(pieces),
        out_specs=[spec(electrons)] + [spec(elec)] * planes,
        out_shape=[shape(electrons)] + [shape(elec)] * planes,
        scratch_shapes=[
            pltpu.VMEM((block, orbitals, orbitals), jnp.bfloat16),
            pltpu.VMEM((block, electrons, orbitals), jnp.bfloat16),
        ],
        compiler_params=pltpu.CompilerParams(vmem_limit_bytes=24 * 2**20),
        cost_estimate=pl.CostEstimate(
            flops=2 * degrees * slots * electrons * orbitals * orbitals,
            bytes_accessed=2 * slots * orbitals * (orbitals + 3 * electrons),
            transcendentals=0,
        ),
    )(place, phi, *pieces)
    return outs[0], outs[1:]


def plane_shards(chunks, walkers, fields, chol_vectors, rotated, send_walker, slot_row):
    slots, electrons, orbitals = walkers.shape
    nchol, rows, _ = chol_vectors.shape
    elec_local = rotated.shape[1]
    devices = orbitals // rows
    planes = devices // inner
    me = lax.axis_index("chol")
    plane, spot = me // inner, me % inner
    scale = field_scale / math.sqrt(nchol)

    def move(x, k, m):
        route = [
            (p * inner + q, (p + k) % planes * inner + (q ^ m))
            for p in range(planes)
            for q in range(inner)
        ]
        return lax.ppermute(x, "chol", route)

    column = jnp.stack([fields] + [move(fields, planes - k, 0) for k in range(1, planes)])
    everyone = jnp.stack([column] + [move(column, 0, m) for m in range(1, inner)])

    branched = branch_walkers(walkers, send_walker, slot_row)

    rot_mine = jnp.transpose(rotated, (1, 0, 2))
    groups = [[p * inner + q for q in range(inner)] for p in range(planes)]
    rot_plane = lax.all_gather(
        rot_mine, "chol", axis=0, tiled=True, axis_index_groups=groups
    )

    sources = [
        ((plane - k) % planes) * inner + (spot ^ m) for m in range(inner) for k in range(planes)
    ]
    place = jnp.stack(sources + [(plane + k) % planes for k in range(planes)]).astype(jnp.int32)

    per = slots // chunks
    news, biases = [], []
    for c in range(chunks):
        part = everyone[:, :, c * per : (c + 1) * per, :]
        made = (
            jnp.einsum("mkpg,gij->mkpij", part, chol_vectors, preferred_element_type=jnp.float32)
            * scale
        ).astype(jnp.bfloat16)
        pieces = [
            made[m, k] if m == 0 and k == 0 else move(made[m, k], k, m)
            for m in range(inner)
            for k in range(planes)
        ]
        new, parts = propagate(branched[c * per : (c + 1) * per], pieces, place, planes)
        news.append(new)
        held = jnp.stack([parts[0]] + [move(parts[k], k, 0) for k in range(1, planes)])
        sums = jnp.einsum("kpej,egj->kpg", held, rot_plane, preferred_element_type=jnp.float32)
        bias = sums[0]
        for k in range(1, planes):
            back = move(sums[k].astype(jnp.bfloat16), planes - k, 0)
            bias = bias + back.astype(jnp.float32)
        biases.append(bias)
    return (jnp.concatenate(news), jnp.concatenate(biases))


def solution(mesh):
    in_specs = (
        P(("grp", "chol"), None, None),
        P(("grp", "chol"), None),
        P(None, "chol", None),
        P(None, "chol", None),
        P(("grp", "chol"), None, None),
        P(("grp", "chol")),
    )
    out_specs = (P(("grp", "chol"), None, None), P(("grp", "chol"), None))
    devices = mesh.shape["chol"]

    def shards(walkers, fields, chol_vectors, rotated, send_walker, slot_row):
        rows = chol_vectors.shape[1]
        plane_elec = walkers.shape[1] * inner // devices
        if devices % inner == 0 and rows % 16 == 0 and plane_elec % 16 == 0:
            body = functools.partial(plane_shards, 2 if walkers.shape[0] % 32 == 0 else 1)
        else:
            body = plain_shards
        return body(walkers, fields, chol_vectors, rotated, send_walker, slot_row)

    return jax.shard_map(shards, mesh=mesh, in_specs=in_specs, out_specs=out_specs, check_vma=False)
```

```python
import functools
import math

import jax
import jax.numpy as jnp
import numpy as np
from jax import lax
from jax.experimental import pallas as pl
from jax.experimental.pallas import tpu as pltpu
from jax.sharding import PartitionSpec as P

field_scale = 1.5
degrees = 5
window = 5
early_walkers = 6
electrons_at = 6
sums_at = 10
inner = 4


def pick_outgoing(walkers, send_walker):
    slots = walkers.shape[0]
    flat_walkers = walkers.reshape(slots, -1)
    send_list = send_walker.reshape(-1)
    choose = (send_list[:, None] == jnp.arange(slots, dtype=jnp.int32)[None, :]).astype(
        jnp.bfloat16
    )
    return jnp.dot(choose, flat_walkers, preferred_element_type=jnp.float32).astype(jnp.bfloat16)


def pick_incoming(incoming, slot_row, names):
    choose = (slot_row[:, None] == names[None, :]).astype(jnp.bfloat16)
    return jnp.dot(choose, incoming, preferred_element_type=jnp.float32).astype(jnp.bfloat16)


def build_operators(fields, chol_vectors):
    nchol, row_local, orbitals = chol_vectors.shape
    chol_flat = chol_vectors.reshape(nchol, row_local * orbitals)
    scale = field_scale / math.sqrt(nchol)
    all_fields = lax.all_gather(fields, "chol", axis=0, tiled=True)
    all_rows = (jnp.dot(all_fields, chol_flat, preferred_element_type=jnp.float32) * scale).astype(
        jnp.bfloat16
    )
    return all_rows.reshape(all_rows.shape[0], row_local, orbitals)


def plain_shards(walkers, fields, chol_vectors, rotated, send_walker, slot_row):
    slots, electrons, orbitals = walkers.shape
    outgoing = pick_outgoing(walkers, send_walker)
    incoming = lax.all_to_all(outgoing, "chol", split_axis=0, concat_axis=0, tiled=True)
    names = jnp.arange(incoming.shape[0], dtype=jnp.int32)
    branched = pick_incoming(incoming, slot_row, names).reshape(slots, electrons, orbitals)
    operator_rows = build_operators(fields, chol_vectors)
    operator = lax.all_to_all(operator_rows, "chol", split_axis=0, concat_axis=1, tiled=True)
    total = branched.astype(jnp.float32)
    term = branched
    for degree in range(1, degrees + 1):
        product = jnp.einsum("waj,wij->wai", term, operator, preferred_element_type=jnp.float32)
        term = (product / degree).astype(jnp.bfloat16)
        total = total + term.astype(jnp.float32)
    new_walkers = total.astype(jnp.bfloat16)
    nchol, elec_local, _ = rotated.shape
    electron_rows = lax.all_to_all(new_walkers, "chol", split_axis=1, concat_axis=0, tiled=True)
    electron_flat = electron_rows.reshape(electron_rows.shape[0], elec_local * orbitals)
    rot_flat = rotated.reshape(nchol, elec_local * orbitals)
    force_bias = lax.psum_scatter(
        lax.dot_general(
            electron_flat, rot_flat, (((1,), (1,)), ((), ())), preferred_element_type=jnp.float32
        ),
        "chol",
        scatter_dimension=0,
        tiled=True,
    )
    return (new_walkers, force_bias)


def propagate_kernel(pieces, planes, rows, elec, place_ref, phi_ref, *refs):
    piece_refs = refs[:pieces]
    new_ref = refs[pieces]
    part_refs = refs[pieces + 1 : pieces + 1 + planes]
    op_ref, done_ref = refs[pieces + 1 + planes :]
    block = phi_ref.shape[0]
    for r in range(pieces):
        at = pl.multiple_of(place_ref[r] * rows, rows)
        op_ref[:, pl.ds(at, rows), :] = piece_refs[r][...]
    terms = [phi_ref[w] for w in range(block)]
    totals = [t.astype(jnp.float32) for t in terms]
    for degree in range(1, degrees + 1):
        for w in range(block):
            product = lax.dot_general(
                terms[w], op_ref[w], (((1,), (1,)), ((), ())), preferred_element_type=jnp.float32
            )
            terms[w] = (product * np.float32(1.0 / degree)).astype(jnp.bfloat16)
            totals[w] = totals[w] + terms[w].astype(jnp.float32)
    for w in range(block):
        out = totals[w].astype(jnp.bfloat16)
        new_ref[w] = out
        done_ref[w] = out
    for k in range(planes):
        at = pl.multiple_of(place_ref[pieces + k] * elec, elec)
        part_refs[k][...] = done_ref[:, pl.ds(at, elec), :]


def propagate(phi, pieces, place, planes):
    slots, electrons, orbitals = phi.shape
    rows = pieces[0].shape[1]
    elec = electrons // planes
    block = 4 if slots % 4 == 0 else 1
    spec = lambda height: pl.BlockSpec((block, height, orbitals), lambda i: (i, 0, 0))
    shape = lambda height: jax.ShapeDtypeStruct((slots, height, orbitals), jnp.bfloat16)
    outs = pl.pallas_call(
        functools.partial(propagate_kernel, len(pieces), planes, rows, elec),
        grid=(slots // block,),
        in_specs=[pl.BlockSpec(memory_space=pltpu.SMEM), spec(electrons)]
        + [spec(rows)] * len(pieces),
        out_specs=[spec(electrons)] + [spec(elec)] * planes,
        out_shape=[shape(electrons)] + [shape(elec)] * planes,
        scratch_shapes=[
            pltpu.VMEM((block, orbitals, orbitals), jnp.bfloat16),
            pltpu.VMEM((block, electrons, orbitals), jnp.bfloat16),
        ],
        compiler_params=pltpu.CompilerParams(vmem_limit_bytes=24 * 2**20),
        cost_estimate=pl.CostEstimate(
            flops=2 * degrees * slots * electrons * orbitals * orbitals,
            bytes_accessed=2 * slots * orbitals * (orbitals + 3 * electrons),
            transcendentals=0,
        ),
    )(place, phi, *pieces)
    return outs[0], outs[1:]


def after(x, *others):
    return lax.optimization_barrier((x, others))[0]


def plane_shards(chunks, walkers, fields, chol_vectors, rotated, send_walker, slot_row):
    slots, electrons, orbitals = walkers.shape
    nchol, rows, _ = chol_vectors.shape
    devices = orbitals // rows
    planes = devices // inner
    me = lax.axis_index("chol")
    plane, spot = me // inner, me % inner
    scale = field_scale / math.sqrt(nchol)
    everywhere = [(k, m) for m in range(inner) for k in range(planes)]
    shifts = sorted(range(planes), key=lambda k: -min(k, planes - k))
    order = [(k, m) for m in range(inner) for k in shifts if (k, m) != (0, 0)]
    sent = []

    def move(x, k, m):
        if len(sent) >= window:
            x = after(x, sent[-window])
        route = [
            (p * inner + q, (p + k) % planes * inner + (q ^ m))
            for p in range(planes)
            for q in range(inner)
        ]
        sent.append(lax.ppermute(x, "chol", route))
        return sent[-1]

    column = jnp.stack([fields] + [move(fields, planes - k, 0) for k in range(1, planes)])
    everyone = jnp.stack([column] + [move(column, 0, m) for m in range(1, inner)])

    targets = jnp.stack([(plane + k) % planes * inner + (spot ^ m) for k, m in everywhere])
    sources = jnp.stack([(plane - k) % planes * inner + (spot ^ m) for k, m in everywhere])
    cap = send_walker.shape[2]
    picked = pick_outgoing(walkers, send_walker[0][targets]).reshape(devices, cap, -1)
    outgoing = {at: picked[i] for i, at in enumerate(everywhere)}
    arrived = {(0, 0): outgoing[0, 0]}

    def send_walkers(count):
        for at in [at for at in order if at not in arrived][:count]:
            arrived[at] = move(outgoing[at], *at)

    rot_mine = after(jnp.transpose(rotated, (1, 0, 2)), everyone)
    groups = [[p * inner + q for q in range(inner)] for p in range(planes)]
    rot_plane = lax.all_gather(
        rot_mine, "chol", axis=0, tiled=True, axis_index_groups=groups
    )
    place = jnp.concatenate([sources, (plane + jnp.arange(planes)) % planes]).astype(jnp.int32)

    def operator_rows(part):
        made = (
            jnp.einsum("mkpg,gij->mkpij", part, chol_vectors, preferred_element_type=jnp.float32)
            * scale
        ).astype(jnp.bfloat16)
        return {(k, m): made[m, k] for k, m in everywhere}

    def propagated(phi, landed):
        return propagate(phi, [landed[at] for at in everywhere], place, planes)

    def send_electrons(parts):
        return jnp.stack([parts[0]] + [move(parts[k], k, 0) for k in range(1, planes)])

    def bias_sums(held):
        return jnp.einsum("kpej,egj->kpg", held, rot_plane, preferred_element_type=jnp.float32)

    def return_sums(sums):
        bias = sums[0]
        for k in range(1, planes):
            bias = bias + move(sums[k].astype(jnp.bfloat16), planes - k, 0).astype(jnp.float32)
        return bias

    send_walkers(early_walkers)
    news, biases = [], []
    first, held, sums, mark = 0, None, None, None
    branched = None
    for c, per in enumerate(chunks):
        part = everyone[:, :, first : first + per, :]
        made = operator_rows(part if mark is None else after(part, mark))
        landed = {(0, 0): made[0, 0]}
        for i, at in enumerate(order):
            landed[at] = move(made[at], *at)
            if c == 0:
                send_walkers(1)
            if i == 4:
                mark = landed[at]
            if c > 0 and i == electrons_at:
                held = send_electrons(parts)
            if c > 0 and i == sums_at:
                biases.append(return_sums(bias_sums(held)))
        if branched is None:
            send_walkers(devices)
            rows_in = jnp.concatenate([arrived[at] for at in everywhere])
            names = (sources[:, None] * cap + jnp.arange(cap, dtype=jnp.int32)).reshape(-1)
            branched = pick_incoming(rows_in, slot_row, names).reshape(walkers.shape)
        new, parts = propagated(branched[first : first + per], landed)
        news.append(new)
        first += per
    biases.append(return_sums(bias_sums(send_electrons(parts))))
    return (jnp.concatenate(news), jnp.concatenate(biases))


def solution(mesh):
    in_specs = (
        P(("grp", "chol"), None, None),
        P(("grp", "chol"), None),
        P(None, "chol", None),
        P(None, "chol", None),
        P(("grp", "chol"), None, None),
        P(("grp", "chol")),
    )
    out_specs = (P(("grp", "chol"), None, None), P(("grp", "chol"), None))
    devices = mesh.shape["chol"]

    def shards(walkers, fields, chol_vectors, rotated, send_walker, slot_row):
        rows = chol_vectors.shape[1]
        plane_elec = walkers.shape[1] * inner // devices
        if devices % inner == 0 and rows % 16 == 0 and plane_elec % 16 == 0:
            slots = walkers.shape[0]
            head = slots * 5 // 8 if slots % 32 == 0 else slots
            body = functools.partial(plane_shards, (head, slots - head) if head < slots else (slots,))
        else:
            body = plain_shards
        return body(walkers, fields, chol_vectors, rotated, send_walker, slot_row)

    return jax.shard_map(shards, mesh=mesh, in_specs=in_specs, out_specs=out_specs, check_vma=False)
```

```python
import functools
import math

import jax
import jax.numpy as jnp
import numpy as np
from jax import lax
from jax.experimental import pallas as pl
from jax.experimental.pallas import tpu as pltpu
from jax.sharding import PartitionSpec as P

field_scale = 1.5
degrees = 5
inner = 4


def branch_walkers(walkers, send_walker, slot_row):
    slots, electrons, orbitals = walkers.shape
    flat_walkers = walkers.reshape(slots, electrons * orbitals)
    send_list = send_walker.reshape(-1)
    choose_send = (send_list[:, None] == jnp.arange(slots, dtype=jnp.int32)[None, :]).astype(
        jnp.bfloat16
    )
    outgoing = jnp.dot(choose_send, flat_walkers, preferred_element_type=jnp.float32).astype(
        jnp.bfloat16
    )
    incoming = lax.all_to_all(outgoing, "chol", split_axis=0, concat_axis=0, tiled=True)
    choose_recv = (
        slot_row[:, None] == jnp.arange(incoming.shape[0], dtype=jnp.int32)[None, :]
    ).astype(jnp.bfloat16)
    branched = jnp.dot(choose_recv, incoming, preferred_element_type=jnp.float32).astype(
        jnp.bfloat16
    )
    return branched.reshape(slots, electrons, orbitals)


def build_operators(fields, chol_vectors):
    nchol, row_local, orbitals = chol_vectors.shape
    chol_flat = chol_vectors.reshape(nchol, row_local * orbitals)
    scale = field_scale / math.sqrt(nchol)
    all_fields = lax.all_gather(fields, "chol", axis=0, tiled=True)
    all_rows = (jnp.dot(all_fields, chol_flat, preferred_element_type=jnp.float32) * scale).astype(
        jnp.bfloat16
    )
    return all_rows.reshape(all_rows.shape[0], row_local, orbitals)


def plain_shards(walkers, fields, chol_vectors, rotated, send_walker, slot_row):
    slots, electrons, orbitals = walkers.shape
    branched = branch_walkers(walkers, send_walker, slot_row)
    operator_rows = build_operators(fields, chol_vectors)
    operator = lax.all_to_all(operator_rows, "chol", split_axis=0, concat_axis=1, tiled=True)
    total = branched.astype(jnp.float32)
    term = branched
    for degree in range(1, degrees + 1):
        product = jnp.einsum("waj,wij->wai", term, operator, preferred_element_type=jnp.float32)
        term = (product / degree).astype(jnp.bfloat16)
        total = total + term.astype(jnp.float32)
    new_walkers = total.astype(jnp.bfloat16)
    nchol, elec_local, _ = rotated.shape
    electron_rows = lax.all_to_all(new_walkers, "chol", split_axis=1, concat_axis=0, tiled=True)
    electron_flat = electron_rows.reshape(electron_rows.shape[0], elec_local * orbitals)
    rot_flat = rotated.reshape(nchol, elec_local * orbitals)
    force_bias = lax.psum_scatter(
        lax.dot_general(
            electron_flat, rot_flat, (((1,), (1,)), ((), ())), preferred_element_type=jnp.float32
        ),
        "chol",
        scatter_dimension=0,
        tiled=True,
    )
    return (new_walkers, force_bias)


def propagate_kernel(pieces, planes, rows, elec, place_ref, phi_ref, *refs):
    piece_refs = refs[:pieces]
    new_ref = refs[pieces]
    part_refs = refs[pieces + 1 : pieces + 1 + planes]
    op_ref, done_ref = refs[pieces + 1 + planes :]
    block = phi_ref.shape[0]
    for r in range(pieces):
        at = pl.multiple_of(place_ref[r] * rows, rows)
        op_ref[:, pl.ds(at, rows), :] = piece_refs[r][...]
    terms = [phi_ref[w] for w in range(block)]
    totals = [t.astype(jnp.float32) for t in terms]
    for degree in range(1, degrees + 1):
        for w in range(block):
            product = lax.dot_general(
                terms[w], op_ref[w], (((1,), (1,)), ((), ())), preferred_element_type=jnp.float32
            )
            terms[w] = (product * np.float32(1.0 / degree)).astype(jnp.bfloat16)
            totals[w] = totals[w] + terms[w].astype(jnp.float32)
    for w in range(block):
        out = totals[w].astype(jnp.bfloat16)
        new_ref[w] = out
        done_ref[w] = out
    for k in range(planes):
        at = pl.multiple_of(place_ref[pieces + k] * elec, elec)
        part_refs[k][...] = done_ref[:, pl.ds(at, elec), :]


def propagate(phi, pieces, place, planes):
    slots, electrons, orbitals = phi.shape
    rows = pieces[0].shape[1]
    elec = electrons // planes
    block = 4 if slots % 4 == 0 else 1
    spec = lambda height: pl.BlockSpec((block, height, orbitals), lambda i: (i, 0, 0))
    shape = lambda height: jax.ShapeDtypeStruct((slots, height, orbitals), jnp.bfloat16)
    outs = pl.pallas_call(
        functools.partial(propagate_kernel, len(pieces), planes, rows, elec),
        grid=(slots // block,),
        in_specs=[pl.BlockSpec(memory_space=pltpu.SMEM), spec(electrons)]
        + [spec(rows)] * len(pieces),
        out_specs=[spec(electrons)] + [spec(elec)] * planes,
        out_shape=[shape(electrons)] + [shape(elec)] * planes,
        scratch_shapes=[
            pltpu.VMEM((block, orbitals, orbitals), jnp.bfloat16),
            pltpu.VMEM((block, electrons, orbitals), jnp.bfloat16),
        ],
        compiler_params=pltpu.CompilerParams(vmem_limit_bytes=24 * 2**20),
        cost_estimate=pl.CostEstimate(
            flops=2 * degrees * slots * electrons * orbitals * orbitals,
            bytes_accessed=2 * slots * orbitals * (orbitals + 3 * electrons),
            transcendentals=0,
        ),
    )(place, phi, *pieces)
    return outs[0], outs[1:]


def after(x, *others):
    return lax.optimization_barrier((x, others))[0]


def plane_shards(chunks, walkers, fields, chol_vectors, rotated, send_walker, slot_row):
    slots, electrons, orbitals = walkers.shape
    nchol, rows, _ = chol_vectors.shape
    elec_local = rotated.shape[1]
    devices = orbitals // rows
    planes = devices // inner
    me = lax.axis_index("chol")
    plane, spot = me // inner, me % inner
    scale = field_scale / math.sqrt(nchol)

    def move(x, k, m):
        route = [
            (p * inner + q, (p + k) % planes * inner + (q ^ m))
            for p in range(planes)
            for q in range(inner)
        ]
        return lax.ppermute(x, "chol", route)

    column = jnp.stack([fields] + [move(fields, planes - k, 0) for k in range(1, planes)])
    everyone = jnp.stack([column] + [move(column, 0, m) for m in range(1, inner)])

    branched = branch_walkers(walkers, send_walker, slot_row)

    rot_mine = after(jnp.transpose(rotated, (1, 0, 2)), everyone)
    rot_pair = jnp.concatenate([rot_mine, move(rot_mine, 0, 1)])

    sources = [
        ((plane - k) % planes) * inner + (spot ^ m) for m in range(inner) for k in range(planes)
    ]
    place = jnp.stack(sources + [(plane + k) % planes for k in range(planes)]).astype(jnp.int32)

    pairs = [(k, m) for m in range(0, inner, 2) for k in range(planes)]
    quarter = electrons // devices

    def send_electrons(parts):
        both = parts.reshape(planes, -1, 2, 2 * quarter, orbitals)
        side = {
            m: lax.dynamic_index_in_dim(both, (spot ^ m) // 2, 2, keepdims=False)
            for m in range(0, inner, 2)
        }
        held = [side[m][k] if (k, m) == (0, 0) else move(side[m][k], k, m) for k, m in pairs]
        held = jnp.stack(held).reshape(len(pairs), -1, 2, quarter, orbitals)
        lanes = [
            lax.dynamic_index_in_dim(held, (spot + odd) % 2, 2, keepdims=False) for odd in range(2)
        ]
        return jnp.concatenate(lanes, 2)

    def return_sums(sums):
        bias = sums[0]
        for at, (k, m) in enumerate(pairs[1:], 1):
            back = move(sums[at].astype(jnp.bfloat16), (planes - k) % planes, m)
            bias = bias + back.astype(jnp.float32)
        return bias

    def bias_sums(held):
        return jnp.einsum("rpej,egj->rpg", held, rot_pair, preferred_element_type=jnp.float32)

    def operator_rows(first, per):
        part = everyone[:, :, first : first + per, :]
        made = jnp.einsum(
            "mkpg,gij->mkpij", part, chol_vectors, preferred_element_type=jnp.float32
        )
        return (made * scale).astype(jnp.bfloat16)

    starts = [sum(chunks[:c]) for c in range(len(chunks))]
    made = [operator_rows(*x) for x in zip(starts, chunks)]
    made = lax.optimization_barrier(made)
    order = [(k, m) for m in range(inner) for k in range(planes) if (k, m) != (0, 0)]
    news, parts = [], []
    for c, per in enumerate(chunks):
        landed = {(0, 0): made[c][0, 0]}
        for k, m in order:
            landed[k, m] = move(made[c][m, k], k, m)
        pieces = [landed[k, m] for m in range(inner) for k in range(planes)]
        phi = branched[starts[c] : starts[c] + per]
        new, part = propagate(phi, pieces, place, planes)
        news.append(new)
        parts.append(jnp.stack(part))
    bias = return_sums(bias_sums(send_electrons(jnp.concatenate(parts, 1))))
    return (jnp.concatenate(news), bias)


def solution(mesh):
    in_specs = (
        P(("grp", "chol"), None, None),
        P(("grp", "chol"), None),
        P(None, "chol", None),
        P(None, "chol", None),
        P(("grp", "chol"), None, None),
        P(("grp", "chol")),
    )
    out_specs = (P(("grp", "chol"), None, None), P(("grp", "chol"), None))
    devices = mesh.shape["chol"]

    def shards(walkers, fields, chol_vectors, rotated, send_walker, slot_row):
        rows = chol_vectors.shape[1]
        plane_elec = walkers.shape[1] * inner // devices
        if devices % inner == 0 and rows % 16 == 0 and plane_elec % 16 == 0:
            slots = walkers.shape[0]
            head = slots * 4 // 8
            chunks = (head, slots - head) if slots % 32 == 0 else (slots,)
            body = functools.partial(plane_shards, chunks)
        else:
            body = plain_shards
        return body(walkers, fields, chol_vectors, rotated, send_walker, slot_row)

    return jax.shard_map(shards, mesh=mesh, in_specs=in_specs, out_specs=out_specs, check_vma=False)
```

```python
import functools
import math

import jax
import jax.numpy as jnp
import numpy as np
from jax import lax
from jax.experimental import pallas as pl
from jax.experimental.pallas import tpu as pltpu
from jax.sharding import PartitionSpec as P

field_scale = 1.5
degrees = 5
next_rows_at = 8
inner = 4


def branch_walkers(walkers, send_walker, slot_row):
    slots, electrons, orbitals = walkers.shape
    flat_walkers = walkers.reshape(slots, electrons * orbitals)
    send_list = send_walker.reshape(-1)
    choose_send = (send_list[:, None] == jnp.arange(slots, dtype=jnp.int32)[None, :]).astype(
        jnp.bfloat16
    )
    outgoing = jnp.dot(choose_send, flat_walkers, preferred_element_type=jnp.float32).astype(
        jnp.bfloat16
    )
    incoming = lax.all_to_all(outgoing, "chol", split_axis=0, concat_axis=0, tiled=True)
    choose_recv = (
        slot_row[:, None] == jnp.arange(incoming.shape[0], dtype=jnp.int32)[None, :]
    ).astype(jnp.bfloat16)
    branched = jnp.dot(choose_recv, incoming, preferred_element_type=jnp.float32).astype(
        jnp.bfloat16
    )
    return branched.reshape(slots, electrons, orbitals)


def build_operators(fields, chol_vectors):
    nchol, row_local, orbitals = chol_vectors.shape
    chol_flat = chol_vectors.reshape(nchol, row_local * orbitals)
    scale = field_scale / math.sqrt(nchol)
    all_fields = lax.all_gather(fields, "chol", axis=0, tiled=True)
    all_rows = (jnp.dot(all_fields, chol_flat, preferred_element_type=jnp.float32) * scale).astype(
        jnp.bfloat16
    )
    return all_rows.reshape(all_rows.shape[0], row_local, orbitals)


def plain_shards(walkers, fields, chol_vectors, rotated, send_walker, slot_row):
    slots, electrons, orbitals = walkers.shape
    branched = branch_walkers(walkers, send_walker, slot_row)
    operator_rows = build_operators(fields, chol_vectors)
    operator = lax.all_to_all(operator_rows, "chol", split_axis=0, concat_axis=1, tiled=True)
    total = branched.astype(jnp.float32)
    term = branched
    for degree in range(1, degrees + 1):
        product = jnp.einsum("waj,wij->wai", term, operator, preferred_element_type=jnp.float32)
        term = (product / degree).astype(jnp.bfloat16)
        total = total + term.astype(jnp.float32)
    new_walkers = total.astype(jnp.bfloat16)
    nchol, elec_local, _ = rotated.shape
    electron_rows = lax.all_to_all(new_walkers, "chol", split_axis=1, concat_axis=0, tiled=True)
    electron_flat = electron_rows.reshape(electron_rows.shape[0], elec_local * orbitals)
    rot_flat = rotated.reshape(nchol, elec_local * orbitals)
    force_bias = lax.psum_scatter(
        lax.dot_general(
            electron_flat, rot_flat, (((1,), (1,)), ((), ())), preferred_element_type=jnp.float32
        ),
        "chol",
        scatter_dimension=0,
        tiled=True,
    )
    return (new_walkers, force_bias)


def propagate_kernel(pieces, planes, rows, elec, place_ref, phi_ref, *refs):
    piece_refs = refs[:pieces]
    new_ref = refs[pieces]
    part_refs = refs[pieces + 1 : pieces + 1 + planes]
    op_ref, done_ref = refs[pieces + 1 + planes :]
    block = phi_ref.shape[0]
    for r in range(pieces):
        at = pl.multiple_of(place_ref[r] * rows, rows)
        op_ref[:, pl.ds(at, rows), :] = piece_refs[r][...]
    terms = [phi_ref[w] for w in range(block)]
    totals = [t.astype(jnp.float32) for t in terms]
    for degree in range(1, degrees + 1):
        for w in range(block):
            product = lax.dot_general(
                terms[w], op_ref[w], (((1,), (1,)), ((), ())), preferred_element_type=jnp.float32
            )
            terms[w] = (product * np.float32(1.0 / degree)).astype(jnp.bfloat16)
            totals[w] = totals[w] + terms[w].astype(jnp.float32)
    for w in range(block):
        out = totals[w].astype(jnp.bfloat16)
        new_ref[w] = out
        done_ref[w] = out
    for k in range(planes):
        at = pl.multiple_of(place_ref[pieces + k] * elec, elec)
        part_refs[k][...] = done_ref[:, pl.ds(at, elec), :]


def propagate(phi, pieces, place, planes):
    slots, electrons, orbitals = phi.shape
    rows = pieces[0].shape[1]
    elec = electrons // planes
    block = 8 if slots % 8 == 0 else 1
    spec = lambda height: pl.BlockSpec((block, height, orbitals), lambda i: (i, 0, 0))
    shape = lambda height: jax.ShapeDtypeStruct((slots, height, orbitals), jnp.bfloat16)
    outs = pl.pallas_call(
        functools.partial(propagate_kernel, len(pieces), planes, rows, elec),
        grid=(slots // block,),
        in_specs=[pl.BlockSpec(memory_space=pltpu.SMEM), spec(electrons)]
        + [spec(rows)] * len(pieces),
        out_specs=[spec(electrons)] + [spec(elec)] * planes,
        out_shape=[shape(electrons)] + [shape(elec)] * planes,
        scratch_shapes=[
            pltpu.VMEM((block, orbitals, orbitals), jnp.bfloat16),
            pltpu.VMEM((block, electrons, orbitals), jnp.bfloat16),
        ],
        compiler_params=pltpu.CompilerParams(vmem_limit_bytes=24 * 2**20),
        cost_estimate=pl.CostEstimate(
            flops=2 * degrees * slots * electrons * orbitals * orbitals,
            bytes_accessed=2 * slots * orbitals * (orbitals + 3 * electrons),
            transcendentals=0,
        ),
    )(place, phi, *pieces)
    return outs[0], outs[1:]


def after(x, *others):
    return lax.optimization_barrier((x, others))[0]


def plane_shards(chunks, walkers, fields, chol_vectors, rotated, send_walker, slot_row):
    slots, electrons, orbitals = walkers.shape
    nchol, rows, _ = chol_vectors.shape
    elec_local = rotated.shape[1]
    devices = orbitals // rows
    planes = devices // inner
    me = lax.axis_index("chol")
    plane, spot = me // inner, me % inner
    scale = field_scale / math.sqrt(nchol)

    def move(x, k, m):
        route = [
            (p * inner + q, (p + k) % planes * inner + (q ^ m))
            for p in range(planes)
            for q in range(inner)
        ]
        return lax.ppermute(x, "chol", route)

    column = jnp.stack([fields] + [move(fields, planes - k, 0) for k in range(1, planes)])
    everyone = jnp.stack([column] + [move(column, 0, m) for m in range(1, inner)])

    branched = branch_walkers(walkers, send_walker, slot_row)

    rot_mine = after(jnp.transpose(rotated, (1, 0, 2)), everyone)
    rot_pair = jnp.concatenate([rot_mine, move(rot_mine, 0, 1)])

    sources = [
        ((plane - k) % planes) * inner + (spot ^ m) for m in range(inner) for k in range(planes)
    ]
    place = jnp.stack(sources + [(plane + k) % planes for k in range(planes)]).astype(jnp.int32)

    pairs = [(k, m) for m in range(0, inner, 2) for k in range(planes)]
    quarter = electrons // devices

    def send_electrons(parts):
        both = parts.reshape(planes, -1, 2, 2 * quarter, orbitals)
        side = {
            m: lax.dynamic_index_in_dim(both, (spot ^ m) // 2, 2, keepdims=False)
            for m in range(0, inner, 2)
        }
        held = [side[m][k] if (k, m) == (0, 0) else move(side[m][k], k, m) for k, m in pairs]
        held = jnp.stack(held).reshape(len(pairs), -1, 2, quarter, orbitals)
        lanes = [
            lax.dynamic_index_in_dim(held, (spot + odd) % 2, 2, keepdims=False) for odd in range(2)
        ]
        return jnp.concatenate(lanes, 2)

    def return_sums(sums):
        bias = sums[0]
        for at, (k, m) in enumerate(pairs[1:], 1):
            back = move(sums[at].astype(jnp.bfloat16), (planes - k) % planes, m)
            bias = bias + back.astype(jnp.float32)
        return bias

    def bias_sums(held):
        return jnp.einsum("rpej,egj->rpg", held, rot_pair, preferred_element_type=jnp.float32)

    def operator_rows(first, per):
        part = everyone[:, :, first : first + per, :]
        made = jnp.einsum(
            "mkpg,gij->mkpij", part, chol_vectors, preferred_element_type=jnp.float32
        )
        return (made * scale).astype(jnp.bfloat16)

    starts = [sum(chunks[:c]) for c in range(len(chunks))]
    made = [operator_rows(*x) for x in zip(starts, chunks)]
    order = [(k, m) for m in range(inner) for k in range(planes) if (k, m) != (0, 0)]
    news, parts = [], []
    for c, per in enumerate(chunks):
        landed = {(0, 0): made[c][0, 0]}
        for at, (k, m) in enumerate(order):
            piece = made[c][m, k]
            if c == 0 and len(chunks) > 1 and at >= next_rows_at:
                piece = after(piece, made[1])
            landed[k, m] = move(piece, k, m)
        pieces = [landed[k, m] for m in range(inner) for k in range(planes)]
        phi = branched[starts[c] : starts[c] + per]
        new, part = propagate(phi, pieces, place, planes)
        news.append(new)
        parts.append(jnp.stack(part))
    bias = return_sums(bias_sums(send_electrons(jnp.concatenate(parts, 1))))
    return (jnp.concatenate(news), bias)


def solution(mesh):
    in_specs = (
        P(("grp", "chol"), None, None),
        P(("grp", "chol"), None),
        P(None, "chol", None),
        P(None, "chol", None),
        P(("grp", "chol"), None, None),
        P(("grp", "chol")),
    )
    out_specs = (P(("grp", "chol"), None, None), P(("grp", "chol"), None))
    devices = mesh.shape["chol"]

    def shards(walkers, fields, chol_vectors, rotated, send_walker, slot_row):
        rows = chol_vectors.shape[1]
        plane_elec = walkers.shape[1] * inner // devices
        if devices % inner == 0 and rows % 16 == 0 and plane_elec % 16 == 0:
            slots = walkers.shape[0]
            head = slots * 4 // 8
            chunks = (head, slots - head) if slots % 32 == 0 else (slots,)
            body = functools.partial(plane_shards, chunks)
        else:
            body = plain_shards
        return body(walkers, fields, chol_vectors, rotated, send_walker, slot_row)

    return jax.shard_map(shards, mesh=mesh, in_specs=in_specs, out_specs=out_specs, check_vma=False)
```

```python
import functools
import math

import jax
import jax.numpy as jnp
import numpy as np
from jax import lax
from jax.experimental import pallas as pl
from jax.experimental.pallas import tpu as pltpu
from jax.sharding import PartitionSpec as P

field_scale = 1.5
degrees = 5
next_rows_at = 8
inner = 4


def branch_walkers(walkers, send_walker, slot_row):
    slots, electrons, orbitals = walkers.shape
    flat_walkers = walkers.reshape(slots, electrons * orbitals)
    send_list = send_walker.reshape(-1)
    choose_send = (send_list[:, None] == jnp.arange(slots, dtype=jnp.int32)[None, :]).astype(
        jnp.bfloat16
    )
    outgoing = jnp.dot(choose_send, flat_walkers, preferred_element_type=jnp.float32).astype(
        jnp.bfloat16
    )
    incoming = lax.all_to_all(outgoing, "chol", split_axis=0, concat_axis=0, tiled=True)
    choose_recv = (
        slot_row[:, None] == jnp.arange(incoming.shape[0], dtype=jnp.int32)[None, :]
    ).astype(jnp.bfloat16)
    branched = jnp.dot(choose_recv, incoming, preferred_element_type=jnp.float32).astype(
        jnp.bfloat16
    )
    return branched.reshape(slots, electrons, orbitals)


def build_operators(fields, chol_vectors):
    nchol, row_local, orbitals = chol_vectors.shape
    chol_flat = chol_vectors.reshape(nchol, row_local * orbitals)
    scale = field_scale / math.sqrt(nchol)
    all_fields = lax.all_gather(fields, "chol", axis=0, tiled=True)
    all_rows = (jnp.dot(all_fields, chol_flat, preferred_element_type=jnp.float32) * scale).astype(
        jnp.bfloat16
    )
    return all_rows.reshape(all_rows.shape[0], row_local, orbitals)


def plain_shards(walkers, fields, chol_vectors, rotated, send_walker, slot_row):
    slots, electrons, orbitals = walkers.shape
    branched = branch_walkers(walkers, send_walker, slot_row)
    operator_rows = build_operators(fields, chol_vectors)
    operator = lax.all_to_all(operator_rows, "chol", split_axis=0, concat_axis=1, tiled=True)
    total = branched.astype(jnp.float32)
    term = branched
    for degree in range(1, degrees + 1):
        product = jnp.einsum("waj,wij->wai", term, operator, preferred_element_type=jnp.float32)
        term = (product / degree).astype(jnp.bfloat16)
        total = total + term.astype(jnp.float32)
    new_walkers = total.astype(jnp.bfloat16)
    nchol, elec_local, _ = rotated.shape
    electron_rows = lax.all_to_all(new_walkers, "chol", split_axis=1, concat_axis=0, tiled=True)
    electron_flat = electron_rows.reshape(electron_rows.shape[0], elec_local * orbitals)
    rot_flat = rotated.reshape(nchol, elec_local * orbitals)
    force_bias = lax.psum_scatter(
        lax.dot_general(
            electron_flat, rot_flat, (((1,), (1,)), ((), ())), preferred_element_type=jnp.float32
        ),
        "chol",
        scatter_dimension=0,
        tiled=True,
    )
    return (new_walkers, force_bias)


def propagate_kernel(pieces, planes, rows, elec, place_ref, phi_ref, *refs):
    piece_refs = refs[:pieces]
    new_ref = refs[pieces]
    part_refs = refs[pieces + 1 : pieces + 1 + planes]
    op_ref, done_ref = refs[pieces + 1 + planes :]
    block = phi_ref.shape[0]
    for r in range(pieces):
        at = pl.multiple_of(place_ref[r] * rows, rows)
        op_ref[:, pl.ds(at, rows), :] = piece_refs[r][...]
    terms = [phi_ref[w] for w in range(block)]
    totals = [t.astype(jnp.float32) for t in terms]
    for degree in range(1, degrees + 1):
        for w in range(block):
            product = lax.dot_general(
                terms[w], op_ref[w], (((1,), (1,)), ((), ())), preferred_element_type=jnp.float32
            )
            terms[w] = (product * np.float32(1.0 / degree)).astype(jnp.bfloat16)
            totals[w] = totals[w] + terms[w].astype(jnp.float32)
    for w in range(block):
        out = totals[w].astype(jnp.bfloat16)
        new_ref[w] = out
        done_ref[w] = out
    for k in range(planes):
        at = pl.multiple_of(place_ref[pieces + k] * elec, elec)
        part_refs[k][...] = done_ref[:, pl.ds(at, elec), :]


def propagate(phi, pieces, place, planes):
    slots, electrons, orbitals = phi.shape
    rows = pieces[0].shape[1]
    elec = electrons // planes
    block = 8 if slots % 8 == 0 else 1
    spec = lambda height: pl.BlockSpec((block, height, orbitals), lambda i: (i, 0, 0))
    shape = lambda height: jax.ShapeDtypeStruct((slots, height, orbitals), jnp.bfloat16)
    outs = pl.pallas_call(
        functools.partial(propagate_kernel, len(pieces), planes, rows, elec),
        grid=(slots // block,),
        in_specs=[pl.BlockSpec(memory_space=pltpu.SMEM), spec(electrons)]
        + [spec(rows)] * len(pieces),
        out_specs=[spec(electrons)] + [spec(elec)] * planes,
        out_shape=[shape(electrons)] + [shape(elec)] * planes,
        scratch_shapes=[
            pltpu.VMEM((block, orbitals, orbitals), jnp.bfloat16),
            pltpu.VMEM((block, electrons, orbitals), jnp.bfloat16),
        ],
        compiler_params=pltpu.CompilerParams(vmem_limit_bytes=24 * 2**20),
        cost_estimate=pl.CostEstimate(
            flops=2 * degrees * slots * electrons * orbitals * orbitals,
            bytes_accessed=2 * slots * orbitals * (orbitals + 3 * electrons),
            transcendentals=0,
        ),
    )(place, phi, *pieces)
    return outs[0], outs[1:]


def after(x, *others):
    return lax.optimization_barrier((x, others))[0]


def plane_shards(chunks, walkers, fields, chol_vectors, rotated, send_walker, slot_row):
    slots, electrons, orbitals = walkers.shape
    nchol, rows, _ = chol_vectors.shape
    elec_local = rotated.shape[1]
    devices = orbitals // rows
    planes = devices // inner
    me = lax.axis_index("chol")
    plane, spot = me // inner, me % inner
    scale = field_scale / math.sqrt(nchol)

    def move(x, k, m):
        route = [
            (p * inner + q, (p + k) % planes * inner + (q ^ m))
            for p in range(planes)
            for q in range(inner)
        ]
        return lax.ppermute(x, "chol", route)

    column = jnp.stack([fields] + [move(fields, planes - k, 0) for k in range(1, planes)])
    everyone = jnp.stack([column] + [move(column, 0, m) for m in range(1, inner)])

    branched = branch_walkers(walkers, send_walker, slot_row)

    rot_mine = after(jnp.transpose(rotated, (1, 0, 2)), everyone)
    rot_pair = jnp.concatenate([rot_mine, move(rot_mine, 0, 1)])

    sources = [
        ((plane - k) % planes) * inner + (spot ^ m) for m in range(inner) for k in range(planes)
    ]
    place = jnp.stack(sources + [(plane + k) % planes for k in range(planes)]).astype(jnp.int32)

    shifts = sorted(range(planes), key=lambda k: -min(k, planes - k))
    pairs = [(0, 0)] + [(k, m) for m in range(0, inner, 2) for k in shifts if (k, m) != (0, 0)]
    quarter = electrons // devices

    def send_electrons(parts):
        both = parts.reshape(planes, -1, 2, 2 * quarter, orbitals)
        side = {
            m: lax.dynamic_index_in_dim(both, (spot ^ m) // 2, 2, keepdims=False)
            for m in range(0, inner, 2)
        }
        held = [side[m][k] if (k, m) == (0, 0) else move(side[m][k], k, m) for k, m in pairs]
        held = jnp.stack(held).reshape(len(pairs), -1, 2, quarter, orbitals)
        lanes = [
            lax.dynamic_index_in_dim(held, (spot + odd) % 2, 2, keepdims=False) for odd in range(2)
        ]
        return jnp.concatenate(lanes, 2)

    def return_sums(sums):
        bias = sums[0]
        for at, (k, m) in enumerate(pairs[1:], 1):
            back = move(sums[at].astype(jnp.bfloat16), (planes - k) % planes, m)
            bias = bias + back.astype(jnp.float32)
        return bias

    def bias_sums(held):
        return jnp.einsum("rpej,egj->rpg", held, rot_pair, preferred_element_type=jnp.float32)

    def operator_rows(first, per):
        part = everyone[:, :, first : first + per, :]
        made = jnp.einsum(
            "mkpg,gij->mkpij", part, chol_vectors, preferred_element_type=jnp.float32
        )
        return (made * scale).astype(jnp.bfloat16)

    starts = [sum(chunks[:c]) for c in range(len(chunks))]
    made = [operator_rows(*x) for x in zip(starts, chunks)]
    order = [(k, m) for m in range(inner) for k in range(planes) if (k, m) != (0, 0)]
    news, parts = [], []
    for c, per in enumerate(chunks):
        landed = {(0, 0): made[c][0, 0]}
        for at, (k, m) in enumerate(order):
            piece = made[c][m, k]
            if c == 0 and len(chunks) > 1 and at >= next_rows_at:
                piece = after(piece, made[1])
            landed[k, m] = move(piece, k, m)
        pieces = [landed[k, m] for m in range(inner) for k in range(planes)]
        phi = branched[starts[c] : starts[c] + per]
        new, part = propagate(phi, pieces, place, planes)
        news.append(new)
        parts.append(jnp.stack(part))
    bias = return_sums(bias_sums(send_electrons(jnp.concatenate(parts, 1))))
    return (jnp.concatenate(news), bias)


def solution(mesh):
    in_specs = (
        P(("grp", "chol"), None, None),
        P(("grp", "chol"), None),
        P(None, "chol", None),
        P(None, "chol", None),
        P(("grp", "chol"), None, None),
        P(("grp", "chol")),
    )
    out_specs = (P(("grp", "chol"), None, None), P(("grp", "chol"), None))
    devices = mesh.shape["chol"]

    def shards(walkers, fields, chol_vectors, rotated, send_walker, slot_row):
        rows = chol_vectors.shape[1]
        plane_elec = walkers.shape[1] * inner // devices
        if devices % inner == 0 and rows % 16 == 0 and plane_elec % 16 == 0:
            slots = walkers.shape[0]
            head = slots * 4 // 8
            chunks = (head, slots - head) if slots % 32 == 0 else (slots,)
            body = functools.partial(plane_shards, chunks)
        else:
            body = plain_shards
        return body(walkers, fields, chol_vectors, rotated, send_walker, slot_row)

    return jax.shard_map(shards, mesh=mesh, in_specs=in_specs, out_specs=out_specs, check_vma=False)
```
